32 devices in a mesh: groups: 2 (over x), expert: 16 (over z, y, core).
Axes of the slice: x: 2, y: 2, z: 4, core: 2. Of those that a mesh axis runs over, the one named last changes fastest.
Arguments:
- tokens: bfloat16 [4096, 3584], P(('groups', 'expert')), parts along dimension 0, may hold values from -6 to 6
- expert_weights: bfloat16 [3, 3584, 8192], P(None, None, 'expert'), may hold values from -0.09375 to 0.09375
- expert_ids: int32 [4096, 2], P(('groups', 'expert')), parts along dimension 0, may hold values from 0 to 7, as said below
- copy_ids: int32 [4096, 2], P(('groups', 'expert')), parts along dimension 0, may hold values from 0 to 1, as said below
- gate_weights: bfloat16 [4096, 2], P(('groups', 'expert')), parts along dimension 0, may hold values from 0.099609375 to 1
Outputs:
- moe_out: bfloat16 [4096, 3584], P(('groups', 'expert')), parts along dimension 0
- served: int32 [32, 2], P(('groups', 'expert')), parts along dimension 0
The draws below stay inside these ranges and needn't reach their ends.
There are 2 independent parts, one for each index of `groups`. The reference program is written for one: setup_inputs(seed, part) draws one part's arguments, and reference() takes and returns one part's arrays. A program takes and returns all parts, laid end to end along the dimension named above; an argument that names none is the same for every part. Nothing has to cross between parts.
Inputs may be any that keep to these rules, and one draw needn't show every extreme that they name: `expert_ids`: each row names 2 different experts. In the rows of one device no expert is named more than 2 * 32 times, and one expert, the same on every device, is named exactly 2 * 32 times in the rows of every device. `copy_ids`: in the rows of one device at most 32 routes name one expert with one slot number; both slots of the expert named 2 * 32 times take exactly 32 routes from every device.
All inputs are finite; a program needn't handle non-finite values.
Results may differ from the reference program's by a relative error of at most 0.0057.
Values may be sent and summed in bfloat16 or wider, within the bound.
No kernel may reach another device: no remote copies, remote signals or barrier semaphores. Data moves between devices by JAX's collectives and lax.ppermute only.
A program may use at most 128 MiB of HBM per device.

```python
import jax
import jax.numpy as jnp
from jax import lax

D = 3584
FF = 1024
TOP = 2
TOK_DEV = 128
EXPERTS = 8
CAP = 32
TOKENS = 2048
HIDDEN_SIZE = 8192
N_EXPERT = 16


def route_plan(key):
    label_key, delta_key, offset_key, order_key = jax.random.split(key, 4)
    relabel = jax.random.permutation(label_key, EXPERTS).astype(jnp.int32)
    deltas = jax.random.randint(delta_key, (N_EXPERT, EXPERTS // 2), -CAP, CAP + 1, dtype=jnp.int32)
    deltas = deltas.at[:, 0].set(CAP)
    counts = jnp.stack([CAP + deltas, CAP - deltas], axis=-1).reshape(N_EXPERT, EXPERTS)
    run_end = jnp.cumsum(counts, axis=1).astype(jnp.int32)
    run_begin = run_end - counts
    places = jnp.arange(TOK_DEV * TOP, dtype=jnp.int32)
    labels = jnp.sum((run_end[:, None, :] <= places[None, :, None]).astype(jnp.int32), axis=2)
    run_rank = places[None, :] - jnp.take_along_axis(run_begin, labels, axis=1)
    offsets = jax.random.randint(offset_key, (N_EXPERT, EXPERTS), 0, 2, dtype=jnp.int32)
    copies = (run_rank + jnp.take_along_axis(offsets, labels, axis=1)) % 2
    experts = relabel[labels]
    experts = experts.reshape(N_EXPERT, TOP, TOK_DEV).transpose(0, 2, 1)
    copies = copies.reshape(N_EXPERT, TOP, TOK_DEV).transpose(0, 2, 1)
    row_keys = jax.random.split(order_key, N_EXPERT)
    shuffles = jax.vmap(lambda single: jax.random.permutation(single, TOK_DEV))(row_keys).astype(jnp.int32)
    experts = jnp.take_along_axis(experts, shuffles[:, :, None], axis=1)
    copies = jnp.take_along_axis(copies, shuffles[:, :, None], axis=1)
    return (experts.reshape(TOKENS, TOP).astype(jnp.int32), copies.reshape(TOKENS, TOP).astype(jnp.int32))


def draw_expert_ids(key, part):
    experts, copies = route_plan(key)
    return experts


def draw_copy_ids(key, part):
    experts, copies = route_plan(key)
    return copies


def block_scale(stream_key, extent, pieces, least, largest):
    def one(dim, parts):
        draws = jax.random.uniform(jax.random.fold_in(jax.random.fold_in(stream_key, 6), dim), (parts,), jnp.float32, least / len(pieces), largest / len(pieces))
        return jnp.repeat(jnp.exp(draws), extent[dim] // parts).reshape((-1,) + (1,) * (len(extent) - dim - 1))

    gain = one(*pieces[0])
    for cut in pieces[1:]:
        gain = gain * one(*cut)
    return gain


def gaussian(key, dims, width, limit, cuts=(), kind=jnp.bfloat16):
    drawn = jax.random.normal(key, dims, jnp.float32) * width
    if len(cuts) > 0:
        drawn = block_scale(key, dims, cuts, -0.22, 0.18) * drawn
    return jnp.clip(drawn, min=-limit, max=limit).astype(kind)


def setup_inputs(seed: int = 0, part: int = 0) -> dict:
    keys = jax.random.split(jax.random.key(seed), 6)
    part_keys = jax.random.split(jax.random.fold_in(keys[5], part), 6)
    tokens = gaussian(part_keys[0], (TOKENS, D), 1.0, 6.0, ((0, 16),))
    expert_weights = gaussian(keys[1], (3, D, HIDDEN_SIZE), D ** -0.5, 0.09375, ((2, 16),))
    expert_ids = draw_expert_ids(jax.random.fold_in(jax.random.fold_in(keys[5], part), 71), part)
    copy_ids = draw_copy_ids(jax.random.fold_in(jax.random.fold_in(keys[5], part), 71), part)
    gate_weights = jnp.clip(0.099609375 + 0.9003906 * jax.random.uniform(part_keys[4], (TOKENS, TOP), jnp.float32) ** block_scale(part_keys[4], (TOKENS, TOP), ((0, 16),), -0.2, 0.2), 0.099609375, 1.0).astype(jnp.bfloat16)
    return {"tokens": tokens, "expert_weights": expert_weights, "expert_ids": expert_ids, "copy_ids": copy_ids, "gate_weights": gate_weights}


def reference(tokens, expert_weights, expert_ids, copy_ids, gate_weights):
    total_rows = tokens.shape[0]
    routes = total_rows * TOP
    flat_expert = expert_ids.reshape(routes).astype(jnp.int32)
    flat_copy = copy_ids.reshape(routes).astype(jnp.int32)
    flat_token = (jnp.arange(routes, dtype=jnp.int32) // TOP).astype(jnp.int32)
    flat_gate = gate_weights.reshape(routes).astype(jnp.float32)
    slot_key = flat_expert * 2 + flat_copy
    key_range = jnp.arange(2 * EXPERTS, dtype=jnp.int32)
    per_slot = jnp.sum((slot_key[:, None] == key_range[None, :]).astype(jnp.int32), axis=0)
    served = jnp.repeat(per_slot.reshape(EXPERTS, 2), 2, axis=0).astype(jnp.int32)

    sorted_routes = jnp.argsort(flat_expert, stable=True).astype(jnp.int32)
    expert_range = jnp.arange(EXPERTS, dtype=jnp.int32)
    counts = jnp.sum((flat_expert[:, None] == expert_range[None, :]).astype(jnp.int32), axis=0)
    starts = (jnp.cumsum(counts) - counts).astype(jnp.int32)
    row_limit = 2 * CAP * N_EXPERT
    slot_range = jnp.arange(row_limit, dtype=jnp.int32)
    padded = jnp.concatenate([tokens, jnp.zeros((1, D), tokens.dtype)], axis=0)
    half_width = FF // 2

    def one_expert(total_out, expert):
        position = starts[expert] + slot_range
        is_live = slot_range < counts[expert]
        route_index = sorted_routes[jnp.clip(position, 0, routes - 1)]
        token_index = jnp.where(is_live, flat_token[route_index], total_rows).astype(jnp.int32)
        row_block = padded[token_index]
        weight = jnp.where(is_live, flat_gate[route_index], jnp.zeros((), jnp.float32))
        summed = jnp.zeros((row_limit, D), jnp.float32)
        for half_index in range(2):
            first_col = (expert * FF + half_index * half_width).astype(jnp.int32)
            columns = lax.dynamic_slice_in_dim(expert_weights, first_col, half_width, 2)
            gate_act = jnp.dot(row_block, columns[0], preferred_element_type=jnp.float32)
            up_act = jnp.dot(row_block, columns[1], preferred_element_type=jnp.float32)
            hidden = (jax.nn.silu(gate_act) * up_act).astype(jnp.bfloat16)
            partial_out = lax.dot_general(hidden, columns[2], (((1,), (1,)), ((), ())), preferred_element_type=jnp.float32)
            summed = summed + partial_out.astype(jnp.bfloat16).astype(jnp.float32)
        total_out = total_out.at[token_index].add(weight[:, None] * summed)
        return total_out, None

    start_out = jnp.zeros((total_rows + 1, D), jnp.float32)
    total_out, _ = lax.scan(one_expert, start_out, expert_range)
    return total_out[:total_rows].astype(jnp.bfloat16), served
```

```python
import jax
import jax.numpy as jnp
from jax import lax
from jax.sharding import PartitionSpec as P

CORES = 2


def grid_of(chips):
    inner = 1
    while (2 * inner) * (2 * inner) <= chips and chips % (2 * inner) == 0:
        inner *= 2
    return chips // inner, inner


def ring_of(length):
    return [p for p in range(length) if p % 2 == 0] + [p for p in reversed(range(length)) if p % 2 == 1]


def hidden_of(rows, weights):
    gate_act = jnp.dot(rows, weights[0], preferred_element_type=jnp.float32)
    up_act = jnp.dot(rows, weights[1], preferred_element_type=jnp.float32)
    return (jax.nn.silu(gate_act) * up_act).astype(jnp.bfloat16)


def down_of(hidden, weights):
    return lax.dot_general(hidden, weights[2], (((1,), (1,)), ((), ())), preferred_element_type=jnp.float32)


def on_device(tokens, expert_weights, expert_ids, copy_ids, gate_weights):
    devices = lax.axis_size("expert")
    experts = devices // CORES
    outer, inner = grid_of(experts)
    tok_rows, top_k = expert_ids.shape
    slots = 2 * (tok_rows * top_k // experts)
    me = lax.axis_index("expert")
    core = me % CORES
    chip = me // CORES
    col = chip % inner
    plane = chip // inner

    ring = ring_of(outer)
    place = jnp.asarray([ring.index(p) for p in range(outer)], jnp.int32)[plane]
    ring_list = jnp.asarray(ring, jnp.int32)

    def device_of(p, q, c):
        return (p * inner + q) * CORES + c

    every = [(p, q, c) for p in range(outer) for q in range(inner) for c in range(CORES)]
    ring_pairs = [
        (device_of(p, q, c), device_of(ring[(ring.index(p) + 1) % outer], q, c)) for p, q, c in every
    ]

    def column_pairs(shift):
        return [(device_of(p, q, c), device_of(p, (q + shift) % inner, c)) for p, q, c in every]

    core_pairs = [(device_of(p, q, c), device_of(p, q, 1 - c)) for p, q, c in every]

    def permute(x, pairs):
        return lax.ppermute(x, "expert", pairs)

    keys = (expert_ids * 2 + copy_ids).astype(jnp.float32)
    meta = jnp.concatenate([keys.T, gate_weights.astype(jnp.float32).T], axis=0)
    metas = lax.all_gather(meta, "expert")
    all_keys = metas[:, :top_k].astype(jnp.int32)
    slot_range = jnp.arange(2, dtype=jnp.int32)
    served = jnp.sum(
        (all_keys[None] == (chip * 2 + slot_range)[:, None, None, None]).astype(jnp.int32), axis=(1, 2, 3)
    ).reshape(1, 2)

    tri = (
        jnp.arange(tok_rows, dtype=jnp.int32)[:, None] <= jnp.arange(tok_rows, dtype=jnp.int32)[None, :]
    ).astype(jnp.float32)
    slot_ids = jnp.arange(slots, dtype=jnp.int32)

    def tables(meta_rows):
        ids = meta_rows[:top_k].astype(jnp.int32) // 2
        gates = meta_rows[top_k:]
        wanted = plane * inner + (col + jnp.arange(inner, dtype=jnp.int32)) % inner
        match = (ids[None] == wanted[:, None, None]).astype(jnp.float32)
        hit = jnp.sum(match, axis=1)
        weight = jnp.sum(match * gates[None], axis=1)
        rank = jnp.dot(hit, tri, preferred_element_type=jnp.float32).astype(jnp.int32) - 1
        onehot = ((rank[:, None, :] == slot_ids[None, :, None]) & (hit[:, None, :] > 0)).astype(jnp.float32)
        pack = onehot.astype(jnp.bfloat16)
        combine = (onehot * weight[:, None, :]).astype(jnp.bfloat16)
        return pack.reshape(inner * slots, tok_rows), combine.reshape(inner * slots, tok_rows)

    blocks = [tokens]
    for step in range(1, outer):
        blocks.append(permute(blocks[-1], ring_pairs))
    other_weights = permute(expert_weights, core_pairs)

    combines, parts = [], []
    for step in range(outer):
        if step == 0:
            source_meta = meta
        else:
            source = device_of(ring_list[(place - step + outer) % outer], col, core)
            source_meta = lax.dynamic_index_in_dim(metas, source, 0, keepdims=False)
        pack, combine = tables(source_meta)
        combines.append(combine)
        packed = jnp.dot(pack, blocks[step], preferred_element_type=jnp.float32).astype(jnp.bfloat16)
        rows = [packed[:slots]]
        for shift in range(1, inner):
            rows.append(permute(packed[shift * slots : (shift + 1) * slots], column_pairs(shift)))
        parts.append(jnp.concatenate(rows, axis=0))

    def run(rows):
        own = hidden_of(rows, expert_weights)
        other = hidden_of(rows, other_weights)
        return (down_of(own, expert_weights) + down_of(other, other_weights)).astype(jnp.bfloat16)

    def send_back(rows):
        back = [rows[:slots]]
        for shift in range(1, inner):
            back.append(permute(rows[shift * slots : (shift + 1) * slots], column_pairs(-shift)))
        return jnp.concatenate(back, axis=0)

    block_rows = inner * slots
    results = [None] * outer
    first = run(jnp.concatenate(parts[:2], axis=0))
    results[0], results[1] = first[:block_rows], first[block_rows:]
    for step in range(2, outer):
        results[step] = run(parts[step])

    carry = None
    for step in list(range(1, outer)) + [0]:
        back = send_back(results[step])
        total = lax.dot_general(
            combines[step], back, (((0,), (0,)), ((), ())), preferred_element_type=jnp.float32
        )
        if carry is not None:
            total = total + carry.astype(jnp.float32)
        total = total.astype(jnp.bfloat16)
        if step != 0:
            carry = permute(total, ring_pairs)
    return total, served


def solution(mesh):
    return jax.shard_map(
        on_device,
        mesh=mesh,
        in_specs=(
            P(("groups", "expert"), None),
            P(None, None, "expert"),
            P(("groups", "expert"), None),
            P(("groups", "expert"), None),
            P(("groups", "expert"), None),
        ),
        out_specs=(P(("groups", "expert"), None), P(("groups", "expert"), None)),
        check_vma=False,
    )
```

```python
import functools

import jax
import jax.numpy as jnp
from jax import lax
from jax.experimental import pallas as pl
from jax.experimental.pallas import tpu as pltpu
from jax.sharding import PartitionSpec as P

CORES = 2
LANES = 128
LARGE_VMEM = 60 * 1024 * 1024
VMEM_LIMIT = 48 * 1024 * 1024
SMALL_VMEM = 16 * 1024 * 1024
CHUNK = 896


def grid_of(chips):
    inner = 1
    while (2 * inner) * (2 * inner) <= chips and chips % (2 * inner) == 0:
        inner *= 2
    return chips // inner, inner


def ring_of(length):
    return [p for p in range(length) if p % 2 == 0] + [p for p in reversed(range(length)) if p % 2 == 1]


def tile_of(size, most):
    tile = most
    while size % tile:
        tile -= 128
    return tile


ANYWHERE = pl.BlockSpec(memory_space=pl.ANY)
WHOLE = pl.BlockSpec(memory_space=pltpu.VMEM)


def rows_cost(rows, width):
    return pl.CostEstimate(flops=2 * rows * width, bytes_accessed=4 * rows * width, transcendentals=0)


def eye_of(size):
    row = lax.broadcasted_iota(jnp.int32, (size, size), 0)
    column = lax.broadcasted_iota(jnp.int32, (size, size), 1)
    return row, column


def label_kernel(tokens_ref, experts_ref, copies_ref, gates_ref, out_ref, experts_scr, copies_scr, gates_scr, sem):
    width = tokens_ref.shape[1]
    top_k, tokens = experts_ref.shape
    moves = [
        pltpu.make_async_copy(experts_ref, experts_scr, sem.at[0]),
        pltpu.make_async_copy(copies_ref, copies_scr, sem.at[1]),
        pltpu.make_async_copy(gates_ref, gates_scr, sem.at[2]),
        pltpu.make_async_copy(tokens_ref, out_ref.at[:, pl.ds(0, width)], sem.at[3]),
    ]
    for move in moves:
        move.start()
    for move in moves[:3]:
        move.wait()
    lane = lax.broadcasted_iota(jnp.int32, (LANES, tokens), 0)
    labels = jnp.zeros((LANES, tokens), jnp.float32)
    for k in range(top_k):
        for i, ref in enumerate((experts_scr, copies_scr, gates_scr)):
            values = jnp.broadcast_to(ref[k : k + 1, :].astype(jnp.float32), (LANES, tokens))
            labels = jnp.where(lane == i * top_k + k, values, labels)
    row, column = eye_of(LANES)
    eye = jnp.where(row == column, 1.0, 0.0).astype(jnp.bfloat16)
    turned = lax.dot_general(
        labels.astype(jnp.bfloat16), eye, (((0,), (0,)), ((), ())), preferred_element_type=jnp.float32
    )
    out_ref[:, width:] = turned.astype(jnp.bfloat16)
    moves[3].wait()


def label_rows(tokens, experts, copies, gates):
    rows, width = tokens.shape
    return pl.pallas_call(
        label_kernel,
        out_shape=jax.ShapeDtypeStruct((rows, width + LANES), jnp.bfloat16),
        in_specs=[ANYWHERE] * 4,
        out_specs=WHOLE,
        scratch_shapes=[
            pltpu.VMEM(experts.shape, experts.dtype),
            pltpu.VMEM(copies.shape, copies.dtype),
            pltpu.VMEM(gates.shape, gates.dtype),
            pltpu.SemaphoreType.DMA((4,)),
        ],
        compiler_params=pltpu.CompilerParams(vmem_limit_bytes=LARGE_VMEM),
        cost_estimate=rows_cost(rows, width),
    )(tokens, experts, copies, gates)


def dispatch_kernel(scalars, block_ref, *refs, inner, top_k, behind):
    rows_refs, combine_ref, counts_ref = refs[behind : behind + inner], refs[behind + inner], refs[behind + inner + 1]
    tokens = block_ref.shape[0]
    slots, width = rows_refs[0].shape
    base, col = scalars[0], scalars[1]
    row, column = eye_of(tokens)
    eye = jnp.where(row == column, 1.0, 0.0).astype(jnp.bfloat16)
    upto = jnp.where(row <= column, 1.0, 0.0).astype(jnp.bfloat16)
    labels = lax.dot_general(
        block_ref[:, width:], eye, (((0,), (0,)), ((), ())), preferred_element_type=jnp.float32
    )
    slot = lax.broadcasted_iota(jnp.int32, (slots, tokens), 0)
    lane = lax.broadcasted_iota(jnp.int32, (1, LANES), 1)
    counts_ref[...] = jnp.zeros_like(counts_ref)
    for j in range(inner):
        wanted = (base + lax.rem(col + j, inner)).astype(jnp.float32)
        hit = jnp.zeros((1, tokens), jnp.float32)
        weight = jnp.zeros((1, tokens), jnp.float32)
        upper = jnp.zeros((1, tokens), jnp.float32)
        for k in range(top_k):
            same = labels[k : k + 1] == wanted
            hit = hit + jnp.where(same, 1.0, 0.0)
            upper = upper + jnp.where(same, labels[top_k + k : top_k + k + 1], 0.0)
            weight = weight + jnp.where(same, labels[2 * top_k + k : 2 * top_k + k + 1], 0.0)
        wide = jnp.broadcast_to(hit, (8, tokens)).astype(jnp.bfloat16)
        rank = jnp.dot(wide, upto, preferred_element_type=jnp.float32)[:1].astype(jnp.int32) - 1
        chosen = (slot == rank) & (hit > 0.5)
        pack = jnp.where(chosen, 1.0, 0.0).astype(jnp.bfloat16)
        combine_ref[j] = jnp.where(chosen, weight, 0.0).astype(jnp.bfloat16)
        rows_refs[j][...] = jnp.dot(pack, block_ref[:, :width], preferred_element_type=jnp.float32).astype(jnp.bfloat16)
        ones = jnp.sum(upper, axis=1, keepdims=True)
        zeros = jnp.sum(hit, axis=1, keepdims=True) - ones
        counts_ref[j : j + 1, :] = jnp.where(lane == 0, zeros, jnp.where(lane == 1, ones, 0.0))


def dispatch_rows(scalars, block, top_k, inner, slots, after=()):
    tokens, width = block.shape
    width -= LANES
    outs = pl.pallas_call(
        functools.partial(dispatch_kernel, inner=inner, top_k=top_k, behind=len(after)),
        out_shape=[jax.ShapeDtypeStruct((slots, width), jnp.bfloat16)] * inner
        + [
            jax.ShapeDtypeStruct((inner, slots, tokens), jnp.bfloat16),
            jax.ShapeDtypeStruct((-(-inner // 8) * 8, LANES), jnp.float32),
        ],
        in_specs=[pl.BlockSpec(memory_space=pltpu.SMEM), WHOLE] + [ANYWHERE] * len(after),
        out_specs=[WHOLE] * (inner + 2),
        compiler_params=pltpu.CompilerParams(vmem_limit_bytes=SMALL_VMEM),
        cost_estimate=rows_cost(tokens, width),
    )(scalars, block, *after)
    return list(outs[:inner]), outs[inner], outs[inner + 1]


def combine_kernel(combine_ref, *refs, inner, carried, behind):
    out_ref = refs[-1]
    total = refs[inner][...].astype(jnp.float32) if carried else None
    for j in range(inner):
        part = lax.dot_general(
            combine_ref[j], refs[j][...], (((0,), (0,)), ((), ())), preferred_element_type=jnp.float32
        )
        total = part if total is None else total + part
    out_ref[...] = total.astype(jnp.bfloat16)


def combine_rows(table, rows, carried=(), after=()):
    inner, _, tokens = table.shape
    width = rows[0].shape[1]
    return pl.pallas_call(
        functools.partial(combine_kernel, inner=inner, carried=len(carried), behind=len(after)),
        out_shape=jax.ShapeDtypeStruct((tokens, width), jnp.bfloat16),
        in_specs=[WHOLE] * (1 + inner + len(carried)) + [ANYWHERE] * len(after),
        out_specs=WHOLE,
        compiler_params=pltpu.CompilerParams(vmem_limit_bytes=SMALL_VMEM),
        cost_estimate=rows_cost(tokens, width),
    )(table, *rows, *carried, *after)


def expert_kernel(*refs, pieces, behind, chunks):
    row_refs = refs[:pieces]
    weights = refs[pieces : pieces + 2]
    out_refs = refs[pieces + 2 + behind : 2 * pieces + 2 + behind]
    rows_scr, hidden_scr, own_scr, other_scr, up_sem, down_sem = refs[2 * pieces + 2 + behind :]
    held = (own_scr, other_scr)
    slots = row_refs[0].shape[0]
    chunk = rows_scr.shape[2]

    def up_copy(half, k):
        part = (pl.ds(0, 2), pl.ds(k * chunk, chunk))
        return pltpu.make_async_copy(weights[half].at[part], held[half].at[part], up_sem.at[half, k])

    def down_copy(half, k):
        part = (pl.ds(2, 1), pl.ds(k * chunk, chunk))
        return pltpu.make_async_copy(weights[half].at[part], held[half].at[part], down_sem.at[half, k])

    for half in range(2):
        for k in range(chunks):
            up_copy(half, k).start()
    for k in range(chunks):
        for half in range(2):
            down_copy(half, k).start()
    for i in range(pieces):
        for k in range(chunks):
            rows_scr[k, i * slots : (i + 1) * slots, :] = row_refs[i][:, k * chunk : (k + 1) * chunk]
    for half in range(2):
        gate_act = up_act = None
        for k in range(chunks):
            up_copy(half, k).wait()
            rows = rows_scr[k]
            gate_part = jnp.dot(rows, held[half][0, k * chunk : (k + 1) * chunk], preferred_element_type=jnp.float32)
            up_part = jnp.dot(rows, held[half][1, k * chunk : (k + 1) * chunk], preferred_element_type=jnp.float32)
            gate_act = gate_part if k == 0 else gate_act + gate_part
            up_act = up_part if k == 0 else up_act + up_part
        hidden_scr[half] = (jax.nn.silu(gate_act) * up_act).astype(jnp.bfloat16)
    for k in range(chunks):
        out = None
        for half in range(2):
            down_copy(half, k).wait()
            part = lax.dot_general(
                hidden_scr[half],
                held[half][2, k * chunk : (k + 1) * chunk],
                (((1,), (1,)), ((), ())),
                preferred_element_type=jnp.float32,
            )
            out = part if half == 0 else out + part
        out = out.astype(jnp.bfloat16)
        for i in range(pieces):
            out_refs[i][:, k * chunk : (k + 1) * chunk] = out[i * slots : (i + 1) * slots]


def expert_rows(pieces, own, other, after=()):
    count = len(pieces)
    slots, width = pieces[0].shape
    units = own.shape[2]
    chunk = tile_of(width, CHUNK)
    chunks = width // chunk
    rows = count * slots
    outs = pl.pallas_call(
        functools.partial(expert_kernel, pieces=count, behind=len(after), chunks=chunks),
        out_shape=[jax.ShapeDtypeStruct((slots, width), jnp.bfloat16)] * count,
        in_specs=[WHOLE] * count + [ANYWHERE] * (2 + len(after)),
        out_specs=[WHOLE] * count,
        scratch_shapes=[
            pltpu.VMEM((chunks, rows, chunk), jnp.bfloat16),
            pltpu.VMEM((2, rows, units), jnp.bfloat16),
            pltpu.VMEM(own.shape, jnp.bfloat16),
            pltpu.VMEM(own.shape, jnp.bfloat16),
            pltpu.SemaphoreType.DMA((2, chunks)),
            pltpu.SemaphoreType.DMA((2, chunks)),
        ],
        compiler_params=pltpu.CompilerParams(vmem_limit_bytes=VMEM_LIMIT),
        cost_estimate=pl.CostEstimate(flops=1000, bytes_accessed=1000, transcendentals=0),
    )(*pieces, own, other, *after)
    return list(outs)


def on_device(tokens, expert_weights, expert_ids, copy_ids, gate_weights):
    devices = lax.axis_size("expert")
    experts = devices // CORES
    outer, inner = grid_of(experts)
    tok_rows, top_k = expert_ids.shape
    slots = -(-2 * (tok_rows * top_k // experts) // 16) * 16
    me = lax.axis_index("expert").astype(jnp.int32)
    chip = lax.div(me, CORES)
    col = lax.rem(chip, inner)
    plane = lax.div(chip, inner)
    ring = ring_of(outer)

    def device_of(p, q, c):
        return (p * inner + q) * CORES + c

    every = [(p, q, c) for p in range(outer) for q in range(inner) for c in range(CORES)]

    def ring_pairs(shift):
        return [
            (device_of(p, q, c), device_of(ring[(ring.index(p) + shift) % outer], q, c)) for p, q, c in every
        ]

    def column_pairs(shift):
        return [(device_of(p, q, c), device_of(p, (q + shift) % inner, c)) for p, q, c in every]

    core_pairs = [(device_of(p, q, c), device_of(p, q, 1 - c)) for p, q, c in every]

    def permute(x, pairs):
        return lax.ppermute(x, "expert", pairs)

    blocks = [label_rows(tokens, expert_ids.T, copy_ids.T, gate_weights.T)]
    scalars = jnp.stack([plane * inner, col])
    other_weights = permute(expert_weights, core_pairs)

    def dispatch(step, after=()):
        rows, table, counts = dispatch_rows(scalars, blocks[step], top_k, inner, slots, after)
        arrived = rows[:1] + [permute(rows[shift], column_pairs(shift)) for shift in range(1, inner)]
        return arrived, table, counts

    def send_back(rows):
        return rows[:1] + [permute(rows[shift], column_pairs(-shift)) for shift in range(1, inner)]

    def run(pieces, after=()):
        return expert_rows(pieces, expert_weights, other_weights, after)

    def behind(x, *others):
        return lax.optimization_barrier((x,) + others)[0]

    def pass_on(step, carry):
        return (permute(combine_rows(sent[step][1], back[step], carry), ring_pairs(1)),)

    sent = {0: dispatch(0)}
    blocks.append(permute(blocks[0], ring_pairs(1)))
    blocks[1] = behind(blocks[1], sent[0][0][-1])
    sent[1] = dispatch(1)
    results = {}
    for step in range(2, outer):
        block = behind(blocks[-1], sent[step - 1][1])
        if step == 3:
            results[1] = run(sent[1][0])
            block = behind(block, results[1][0])
        blocks.append(permute(block, ring_pairs(1)))
        if step == 3:
            results[2] = run(sent[2][0])
            blocks[3] = behind(blocks[3], results[2][0])
        sent[step] = dispatch(step)
    for step in list(range(1, outer)) + [0]:
        if step not in results:
            pieces = sent[step][0]
            if step == 2 and outer > 3 and False:
                pieces = [behind(pieces[0], sent[3][1])] + pieces[1:]
            if step == 0:
                pieces = [behind(pieces[0], results[outer - 1][0])] + pieces[1:]
            results[step] = run(pieces)
    back = {}
    for step in range(outer):
        back[step] = send_back(results[step])
    carry = ()
    for step in range(1, outer):
        carry = pass_on(step, carry)
    moe_out = combine_rows(sent[0][1], back[0], carry)

    counts = sum(sent[step][2] for step in range(outer))
    counts = counts + permute(counts, core_pairs)
    served = counts[:1]
    for shift in range(1, inner):
        served = served + permute(counts[shift : shift + 1], column_pairs(shift))
    return moe_out, served[:, :2].astype(jnp.int32)


def solution(mesh):
    return jax.shard_map(
        on_device,
        mesh=mesh,
        in_specs=(
            P(("groups", "expert"), None),
            P(None, None, "expert"),
            P(("groups", "expert"), None),
            P(("groups", "expert"), None),
            P(("groups", "expert"), None),
        ),
        out_specs=(P(("groups", "expert"), None), P(("groups", "expert"), None)),
        check_vma=False,
    )
```

```python
import functools

import jax
import jax.numpy as jnp
from jax import lax
from jax.experimental import pallas as pl
from jax.experimental.pallas import tpu as pltpu
from jax.sharding import PartitionSpec as P

CORES = 2
LANES = 128
PARTS = 2
LARGE_VMEM = 60 * 1024 * 1024
VMEM_LIMIT = 48 * 1024 * 1024
SMALL_VMEM = 16 * 1024 * 1024
CHUNK = 896


def grid_of(chips):
    inner = 1
    while (2 * inner) * (2 * inner) <= chips and chips % (2 * inner) == 0:
        inner *= 2
    return chips // inner, inner


def ring_of(length):
    return [p for p in range(length) if p % 2 == 0] + [p for p in reversed(range(length)) if p % 2 == 1]


def tile_of(size, most):
    tile = most
    while size % tile:
        tile -= 128
    return tile


ANYWHERE = pl.BlockSpec(memory_space=pl.ANY)
WHOLE = pl.BlockSpec(memory_space=pltpu.VMEM)


def rows_cost(rows, width):
    return pl.CostEstimate(flops=2 * rows * width, bytes_accessed=4 * rows * width, transcendentals=0)


def eye_of(size):
    row = lax.broadcasted_iota(jnp.int32, (size, size), 0)
    column = lax.broadcasted_iota(jnp.int32, (size, size), 1)
    return row, column


def label_kernel(tokens_ref, experts_ref, copies_ref, gates_ref, *refs):
    out_refs, (experts_scr, copies_scr, gates_scr, sem) = refs[:PARTS], refs[PARTS:]
    width = tokens_ref.shape[1] // PARTS
    top_k, tokens = experts_ref.shape
    moves = [
        pltpu.make_async_copy(experts_ref, experts_scr, sem.at[0]),
        pltpu.make_async_copy(copies_ref, copies_scr, sem.at[1]),
        pltpu.make_async_copy(gates_ref, gates_scr, sem.at[2]),
    ]
    for i in range(PARTS):
        part = tokens_ref.at[:, pl.ds(i * width, width)]
        moves.append(pltpu.make_async_copy(part, out_refs[i].at[:, pl.ds(0, width)], sem.at[3 + i]))
    for move in moves:
        move.start()
    for move in moves[:3]:
        move.wait()
    lane = lax.broadcasted_iota(jnp.int32, (LANES, tokens), 0)
    labels = jnp.zeros((LANES, tokens), jnp.float32)
    for k in range(top_k):
        for i, ref in enumerate((experts_scr, copies_scr, gates_scr)):
            values = jnp.broadcast_to(ref[k : k + 1, :].astype(jnp.float32), (LANES, tokens))
            labels = jnp.where(lane == i * top_k + k, values, labels)
    row, column = eye_of(LANES)
    eye = jnp.where(row == column, 1.0, 0.0).astype(jnp.bfloat16)
    turned = lax.dot_general(
        labels.astype(jnp.bfloat16), eye, (((0,), (0,)), ((), ())), preferred_element_type=jnp.float32
    )
    out_refs[0][:, width:] = turned.astype(jnp.bfloat16)
    for move in moves[3:]:
        move.wait()


def label_rows(tokens, experts, copies, gates):
    rows, width = tokens.shape
    part = width // PARTS
    return list(
        pl.pallas_call(
            label_kernel,
            out_shape=[
                jax.ShapeDtypeStruct((rows, part + (0 if i else LANES)), jnp.bfloat16) for i in range(PARTS)
            ],
            in_specs=[ANYWHERE] * 4,
            out_specs=[WHOLE] * PARTS,
            scratch_shapes=[
                pltpu.VMEM(experts.shape, experts.dtype),
                pltpu.VMEM(copies.shape, copies.dtype),
                pltpu.VMEM(gates.shape, gates.dtype),
                pltpu.SemaphoreType.DMA((3 + PARTS,)),
            ],
            compiler_params=pltpu.CompilerParams(vmem_limit_bytes=LARGE_VMEM),
            cost_estimate=rows_cost(rows, width),
        )(tokens, experts, copies, gates)
    )


def dispatch_kernel(scalars, block_ref, *refs, inner, top_k):
    rows_refs, (pack_ref, combine_ref, counts_ref) = refs[:inner], refs[inner:]
    tokens = block_ref.shape[0]
    slots, width = rows_refs[0].shape
    base, col = scalars[0], scalars[1]
    row, column = eye_of(tokens)
    eye = jnp.where(row == column, 1.0, 0.0).astype(jnp.bfloat16)
    upto = jnp.where(row <= column, 1.0, 0.0).astype(jnp.bfloat16)
    labels = lax.dot_general(
        block_ref[:, width:], eye, (((0,), (0,)), ((), ())), preferred_element_type=jnp.float32
    )
    slot = lax.broadcasted_iota(jnp.int32, (slots, tokens), 0)
    lane = lax.broadcasted_iota(jnp.int32, (1, LANES), 1)
    counts_ref[...] = jnp.zeros_like(counts_ref)
    for j in range(inner):
        wanted = (base + lax.rem(col + j, inner)).astype(jnp.float32)
        hit = jnp.zeros((1, tokens), jnp.float32)
        weight = jnp.zeros((1, tokens), jnp.float32)
        upper = jnp.zeros((1, tokens), jnp.float32)
        for k in range(top_k):
            same = labels[k : k + 1] == wanted
            hit = hit + jnp.where(same, 1.0, 0.0)
            upper = upper + jnp.where(same, labels[top_k + k : top_k + k + 1], 0.0)
            weight = weight + jnp.where(same, labels[2 * top_k + k : 2 * top_k + k + 1], 0.0)
        wide = jnp.broadcast_to(hit, (8, tokens)).astype(jnp.bfloat16)
        rank = jnp.dot(wide, upto, preferred_element_type=jnp.float32)[:1].astype(jnp.int32) - 1
        chosen = (slot == rank) & (hit > 0.5)
        pack = jnp.where(chosen, 1.0, 0.0).astype(jnp.bfloat16)
        pack_ref[j] = pack
        combine_ref[j] = jnp.where(chosen, weight, 0.0).astype(jnp.bfloat16)
        rows_refs[j][...] = jnp.dot(pack, block_ref[:, :width], preferred_element_type=jnp.float32).astype(jnp.bfloat16)
        ones = jnp.sum(upper, axis=1, keepdims=True)
        zeros = jnp.sum(hit, axis=1, keepdims=True) - ones
        counts_ref[j : j + 1, :] = jnp.where(lane == 0, zeros, jnp.where(lane == 1, ones, 0.0))


def dispatch_rows(scalars, block, top_k, inner, slots):
    tokens, width = block.shape
    width -= LANES
    table = jax.ShapeDtypeStruct((inner, slots, tokens), jnp.bfloat16)
    outs = pl.pallas_call(
        functools.partial(dispatch_kernel, inner=inner, top_k=top_k),
        out_shape=[jax.ShapeDtypeStruct((slots, width), jnp.bfloat16)] * inner
        + [table, table, jax.ShapeDtypeStruct((-(-inner // 8) * 8, LANES), jnp.float32)],
        in_specs=[pl.BlockSpec(memory_space=pltpu.SMEM), WHOLE],
        out_specs=[WHOLE] * (inner + 3),
        compiler_params=pltpu.CompilerParams(vmem_limit_bytes=SMALL_VMEM),
        cost_estimate=rows_cost(tokens, width),
    )(scalars, block)
    return list(outs[:inner]), outs[inner], outs[inner + 1], outs[inner + 2]


def pack_kernel(pack_ref, block_ref, *rows_refs):
    for j, rows_ref in enumerate(rows_refs):
        rows_ref[...] = jnp.dot(pack_ref[j], block_ref[...], preferred_element_type=jnp.float32).astype(jnp.bfloat16)


def pack_rows(pack, block):
    inner, slots, tokens = pack.shape
    width = block.shape[1]
    return list(
        pl.pallas_call(
            pack_kernel,
            out_shape=[jax.ShapeDtypeStruct((slots, width), jnp.bfloat16)] * inner,
            in_specs=[WHOLE] * 2,
            out_specs=[WHOLE] * inner,
            compiler_params=pltpu.CompilerParams(vmem_limit_bytes=SMALL_VMEM),
            cost_estimate=rows_cost(tokens, width),
        )(pack, block)
    )


def combine_kernel(combine_ref, *refs, inner, parts, carried):
    out_ref = refs[-1]
    width = refs[0].shape[1]
    for i in range(parts):
        total = refs[parts * inner + i][...].astype(jnp.float32) if carried else None
        for j in range(inner):
            part = lax.dot_general(
                combine_ref[j], refs[i * inner + j][...], (((0,), (0,)), ((), ())), preferred_element_type=jnp.float32
            )
            total = part if total is None else total + part
        out_ref[:, i * width : (i + 1) * width] = total.astype(jnp.bfloat16)


def combine_rows(table, rows, carried):
    inner, _, tokens = table.shape
    parts = len(rows)
    width = parts * rows[0][0].shape[1]
    flat = sum(rows, [])
    return pl.pallas_call(
        functools.partial(combine_kernel, inner=inner, parts=parts, carried=len(carried)),
        out_shape=jax.ShapeDtypeStruct((tokens, width), jnp.bfloat16),
        in_specs=[WHOLE] * (1 + len(flat) + len(carried)),
        out_specs=WHOLE,
        compiler_params=pltpu.CompilerParams(vmem_limit_bytes=SMALL_VMEM),
        cost_estimate=rows_cost(tokens, width),
    )(table, *flat, *carried)


def expert_kernel(*refs, pieces, chunks):
    count = pieces * PARTS
    row_refs, weights, out_refs = refs[:count], refs[count : count + 2], refs[count + 2 : 2 * count + 2]
    rows_scr, hidden_scr, own_scr, other_scr, up_sem, down_sem = refs[2 * count + 2 :]
    held = (own_scr, other_scr)
    slots = row_refs[0].shape[0]
    chunk = rows_scr.shape[2]

    def up_copy(half, k):
        part = (pl.ds(0, 2), pl.ds(k * chunk, chunk))
        return pltpu.make_async_copy(weights[half].at[part], held[half].at[part], up_sem.at[half, k])

    def down_copy(half, k):
        part = (pl.ds(2, 1), pl.ds(k * chunk, chunk))
        return pltpu.make_async_copy(weights[half].at[part], held[half].at[part], down_sem.at[half, k])

    for half in range(2):
        for k in range(chunks):
            up_copy(half, k).start()
    for k in range(chunks):
        for half in range(2):
            down_copy(half, k).start()
    for i in range(pieces):
        for k in range(chunks):
            part, k_in = divmod(k, chunks // PARTS)
            source = row_refs[i * PARTS + part]
            rows_scr[k, i * slots : (i + 1) * slots, :] = source[:, k_in * chunk : (k_in + 1) * chunk]
    for half in range(2):
        gate_act = up_act = None
        for k in range(chunks):
            up_copy(half, k).wait()
            rows = rows_scr[k]
            gate_part = jnp.dot(rows, held[half][0, k * chunk : (k + 1) * chunk], preferred_element_type=jnp.float32)
            up_part = jnp.dot(rows, held[half][1, k * chunk : (k + 1) * chunk], preferred_element_type=jnp.float32)
            gate_act = gate_part if k == 0 else gate_act + gate_part
            up_act = up_part if k == 0 else up_act + up_part
        hidden_scr[half] = (jax.nn.silu(gate_act) * up_act).astype(jnp.bfloat16)
    for k in range(chunks):
        out = None
        for half in range(2):
            down_copy(half, k).wait()
            part = lax.dot_general(
                hidden_scr[half],
                held[half][2, k * chunk : (k + 1) * chunk],
                (((1,), (1,)), ((), ())),
                preferred_element_type=jnp.float32,
            )
            out = part if half == 0 else out + part
        out = out.astype(jnp.bfloat16)
        for i in range(pieces):
            part, k_in = divmod(k, chunks // PARTS)
            target = out_refs[i * PARTS + part]
            target[:, k_in * chunk : (k_in + 1) * chunk] = out[i * slots : (i + 1) * slots]


def expert_rows(pieces, own, other):
    count = len(pieces)
    slots, part = pieces[0][0].shape
    units = own.shape[2]
    chunk = tile_of(part, CHUNK)
    chunks = PARTS * part // chunk
    rows = count * slots
    outs = pl.pallas_call(
        functools.partial(expert_kernel, pieces=count, chunks=chunks),
        out_shape=[jax.ShapeDtypeStruct((slots, part), jnp.bfloat16)] * (count * PARTS),
        in_specs=[WHOLE] * (count * PARTS) + [ANYWHERE] * 2,
        out_specs=[WHOLE] * (count * PARTS),
        scratch_shapes=[
            pltpu.VMEM((chunks, rows, chunk), jnp.bfloat16),
            pltpu.VMEM((2, rows, units), jnp.bfloat16),
            pltpu.VMEM(own.shape, jnp.bfloat16),
            pltpu.VMEM(own.shape, jnp.bfloat16),
            pltpu.SemaphoreType.DMA((2, chunks)),
            pltpu.SemaphoreType.DMA((2, chunks)),
        ],
        compiler_params=pltpu.CompilerParams(vmem_limit_bytes=VMEM_LIMIT),
        cost_estimate=pl.CostEstimate(flops=1000, bytes_accessed=1000, transcendentals=0),
    )(*sum(pieces, []), own, other)
    return [list(outs[i * PARTS : (i + 1) * PARTS]) for i in range(count)]


def on_device(tokens, expert_weights, expert_ids, copy_ids, gate_weights):
    devices = lax.axis_size("expert")
    experts = devices // CORES
    outer, inner = grid_of(experts)
    tok_rows, top_k = expert_ids.shape
    slots = -(-2 * (tok_rows * top_k // experts) // 16) * 16
    me = lax.axis_index("expert").astype(jnp.int32)
    chip = lax.div(me, CORES)
    col = lax.rem(chip, inner)
    plane = lax.div(chip, inner)
    ring = ring_of(outer)

    def device_of(p, q, c):
        return (p * inner + q) * CORES + c

    every = [(p, q, c) for p in range(outer) for q in range(inner) for c in range(CORES)]

    def ring_pairs(shift):
        return [
            (device_of(p, q, c), device_of(ring[(ring.index(p) + shift) % outer], q, c)) for p, q, c in every
        ]

    def column_pairs(shift):
        return [(device_of(p, q, c), device_of(p, (q + shift) % inner, c)) for p, q, c in every]

    core_pairs = [(device_of(p, q, c), device_of(p, q, 1 - c)) for p, q, c in every]

    def permute(x, pairs):
        return lax.ppermute(x, "expert", pairs)

    scalars = jnp.stack([plane * inner, col])

    def behind(x, *others):
        return lax.optimization_barrier((x,) + others)[0] if others else x

    def swap(rows, sign):
        return rows[:1] + [permute(rows[shift], column_pairs(sign * shift)) for shift in range(1, inner)]

    def run(pieces):
        return expert_rows(pieces, expert_weights, other_weights)

    def transposed(lists):
        return [list(group) for group in zip(*lists)]

    last = outer - 1
    packs, tables, counts = [None] * outer, [None] * outer, [None] * outer
    packed = [[None] * PARTS for _ in range(outer)]
    sent = [[None] * PARTS for _ in range(outer)]
    results, back, sums = [None] * outer, [None] * outer, [None] * outer
    carry = [()] * PARTS

    def dispatch(step, i, block):
        if i == 0:
            packed[step][0], packs[step], tables[step], counts[step] = dispatch_rows(scalars, block, top_k, inner, slots)
        else:
            packed[step][i] = pack_rows(packs[step], block)
        sent[step][i] = swap(packed[step][i], 1)

    def give_back(step, *others):
        parts = transposed(results[step])
        parts[0] = parts[0][:1] + [behind(x, *others) for x in parts[0][1:]]
        back[step] = [swap(rows, -1) for rows in parts]

    def pass_on(step, gates):
        sums[step] = []
        for i in range(PARTS):
            table = behind(tables[step], *gates[i])
            sums[step].append(combine_rows(table, [back[step][i]], carry[i]))
            carry[i] = (permute(sums[step][i], ring_pairs(1)),)

    none = ((),) * PARTS
    block = label_rows(tokens, expert_ids.T, copy_ids.T, gate_weights.T)
    other_weights = permute(expert_weights, core_pairs)
    for i in range(PARTS):
        dispatch(0, i, block[i])
    block = [permute(part, ring_pairs(1)) for part in block]
    for step in range(1, outer):
        onward = []
        for i in range(PARTS):
            here, gates = block[i], ()
            if step == 1 and i == 0:
                gates = tuple(sent[0][j][-1] for j in range(PARTS))
            if step == 2 and i == 1:
                pieces = transposed(sent[1])
                pieces[0][0] = behind(pieces[0][0], tables[2])
                results[1] = run(pieces)
                here = behind(here, results[1][0][0])
                gates = (results[1][0][0],)
            dispatch(step, i, here)
            if step == 1 and i > 0:
                gates = (packed[1][i][0], sent[1][i - 1][-1])
            if step < last:
                onward.append(permute(behind(block[i], *gates), ring_pairs(1)))
        block = onward
    give_back(1, sent[2][0][-1])
    pass_on(1, ((packed[2][-1][0],),) + ((sent[2][-1][-1],),) * (PARTS - 1))
    routes = sum(counts)
    routes = routes + permute(routes, core_pairs)
    served = routes[:1]
    for shift in range(1, inner):
        served = served + permute(routes[shift : shift + 1], column_pairs(shift))
    for step in range(2, outer):
        pieces = transposed(sent[step])
        gates = (sums[step - 1][-1],)
        if step == 2 and last > 2:
            gates += (packed[3][-1][0],)
        pieces[0][0] = behind(pieces[0][0], *gates)
        if step == last:
            pieces = pieces + transposed(sent[0])
        results[step] = run(pieces)
        gates = none
        if step == last:
            results[0], results[step] = results[step][inner:], results[step][:inner]
            give_back(step)
            give_back(0, *(back[step][i][-1] for i in range(PARTS)))
        elif step == 2:
            give_back(step, carry[0][0], *(sent[3][i][-1] for i in range(PARTS)))
        else:
            give_back(step)
        pass_on(step, gates)
    moe_out = combine_rows(tables[0], back[0], sum(carry, ()))

    return moe_out, served[:, :2].astype(jnp.int32)


def solution(mesh):
    return jax.shard_map(
        on_device,
        mesh=mesh,
        in_specs=(
            P(("groups", "expert"), None),
            P(None, None, "expert"),
            P(("groups", "expert"), None),
            P(("groups", "expert"), None),
            P(("groups", "expert"), None),
        ),
        out_specs=(P(("groups", "expert"), None), P(("groups", "expert"), None)),
        check_vma=False,
    )
```

```python
import functools

import jax
import jax.numpy as jnp
from jax import lax
from jax.experimental import pallas as pl
from jax.experimental.pallas import tpu as pltpu
from jax.sharding import PartitionSpec as P

CORES = 2
LANES = 128
PARTS = 2
LARGE_VMEM = 60 * 1024 * 1024
VMEM_LIMIT = 48 * 1024 * 1024
SMALL_VMEM = 16 * 1024 * 1024
CHUNK = 896


def grid_of(chips):
    inner = 1
    while (2 * inner) * (2 * inner) <= chips and chips % (2 * inner) == 0:
        inner *= 2
    return chips // inner, inner


def ring_of(length):
    return [p for p in range(length) if p % 2 == 0] + [p for p in reversed(range(length)) if p % 2 == 1]


def tile_of(size, most):
    tile = most
    while size % tile:
        tile -= 128
    return tile


ANYWHERE = pl.BlockSpec(memory_space=pl.ANY)
WHOLE = pl.BlockSpec(memory_space=pltpu.VMEM)


def rows_cost(rows, width):
    return pl.CostEstimate(flops=2 * rows * width, bytes_accessed=4 * rows * width, transcendentals=0)


def eye_of(size):
    row = lax.broadcasted_iota(jnp.int32, (size, size), 0)
    column = lax.broadcasted_iota(jnp.int32, (size, size), 1)
    return row, column


def label_kernel(tokens_ref, experts_ref, copies_ref, gates_ref, *refs):
    out_refs, (experts_scr, copies_scr, gates_scr, sem) = refs[:PARTS], refs[PARTS:]
    width = tokens_ref.shape[1] // PARTS
    top_k, tokens = experts_ref.shape
    moves = [
        pltpu.make_async_copy(experts_ref, experts_scr, sem.at[0]),
        pltpu.make_async_copy(copies_ref, copies_scr, sem.at[1]),
        pltpu.make_async_copy(gates_ref, gates_scr, sem.at[2]),
    ]
    for i in range(PARTS):
        part = tokens_ref.at[:, pl.ds(i * width, width)]
        moves.append(pltpu.make_async_copy(part, out_refs[i].at[:, pl.ds(0, width)], sem.at[3 + i]))
    for move in moves:
        move.start()
    for move in moves[:3]:
        move.wait()
    lane = lax.broadcasted_iota(jnp.int32, (LANES, tokens), 0)
    labels = jnp.zeros((LANES, tokens), jnp.float32)
    for k in range(top_k):
        for i, ref in enumerate((experts_scr, copies_scr, gates_scr)):
            values = jnp.broadcast_to(ref[k : k + 1, :].astype(jnp.float32), (LANES, tokens))
            labels = jnp.where(lane == i * top_k + k, values, labels)
    row, column = eye_of(LANES)
    eye = jnp.where(row == column, 1.0, 0.0).astype(jnp.bfloat16)
    turned = lax.dot_general(
        labels.astype(jnp.bfloat16), eye, (((0,), (0,)), ((), ())), preferred_element_type=jnp.float32
    )
    out_refs[0][:, width:] = turned.astype(jnp.bfloat16)
    for move in moves[3:]:
        move.wait()


def label_rows(tokens, experts, copies, gates):
    rows, width = tokens.shape
    part = width // PARTS
    return list(
        pl.pallas_call(
            label_kernel,
            out_shape=[
                jax.ShapeDtypeStruct((rows, part + (0 if i else LANES)), jnp.bfloat16) for i in range(PARTS)
            ],
            in_specs=[ANYWHERE] * 4,
            out_specs=[WHOLE] * PARTS,
            scratch_shapes=[
                pltpu.VMEM(experts.shape, experts.dtype),
                pltpu.VMEM(copies.shape, copies.dtype),
                pltpu.VMEM(gates.shape, gates.dtype),
                pltpu.SemaphoreType.DMA((3 + PARTS,)),
            ],
            compiler_params=pltpu.CompilerParams(vmem_limit_bytes=LARGE_VMEM),
            cost_estimate=rows_cost(rows, width),
        )(tokens, experts, copies, gates)
    )


def dispatch_kernel(scalars, block_ref, *refs, inner, top_k):
    rows_refs, (pack_ref, combine_ref, counts_ref) = refs[:inner], refs[inner:]
    tokens = block_ref.shape[0]
    slots, width = rows_refs[0].shape
    base, col = scalars[0], scalars[1]
    row, column = eye_of(tokens)
    eye = jnp.where(row == column, 1.0, 0.0).astype(jnp.bfloat16)
    upto = jnp.where(row <= column, 1.0, 0.0).astype(jnp.bfloat16)
    labels = lax.dot_general(
        block_ref[:, width:], eye, (((0,), (0,)), ((), ())), preferred_element_type=jnp.float32
    )
    slot = lax.broadcasted_iota(jnp.int32, (slots, tokens), 0)
    lane = lax.broadcasted_iota(jnp.int32, (1, LANES), 1)
    counts_ref[...] = jnp.zeros_like(counts_ref)
    for j in range(inner):
        wanted = (base + lax.rem(col + j, inner)).astype(jnp.float32)
        hit = jnp.zeros((1, tokens), jnp.float32)
        weight = jnp.zeros((1, tokens), jnp.float32)
        upper = jnp.zeros((1, tokens), jnp.float32)
        for k in range(top_k):
            same = labels[k : k + 1] == wanted
            hit = hit + jnp.where(same, 1.0, 0.0)
            upper = upper + jnp.where(same, labels[top_k + k : top_k + k + 1], 0.0)
            weight = weight + jnp.where(same, labels[2 * top_k + k : 2 * top_k + k + 1], 0.0)
        wide = jnp.broadcast_to(hit, (8, tokens)).astype(jnp.bfloat16)
        rank = jnp.dot(wide, upto, preferred_element_type=jnp.float32)[:1].astype(jnp.int32) - 1
        chosen = (slot == rank) & (hit > 0.5)
        pack = jnp.where(chosen, 1.0, 0.0).astype(jnp.bfloat16)
        pack_ref[j] = pack
        combine_ref[j] = jnp.where(chosen, weight, 0.0).astype(jnp.bfloat16)
        rows_refs[j][...] = jnp.dot(pack, block_ref[:, :width], preferred_element_type=jnp.float32).astype(jnp.bfloat16)
        ones = jnp.sum(upper, axis=1, keepdims=True)
        zeros = jnp.sum(hit, axis=1, keepdims=True) - ones
        counts_ref[j : j + 1, :] = jnp.where(lane == 0, zeros, jnp.where(lane == 1, ones, 0.0))


def dispatch_rows(scalars, block, top_k, inner, slots):
    tokens, width = block.shape
    width -= LANES
    table = jax.ShapeDtypeStruct((inner, slots, tokens), jnp.bfloat16)
    outs = pl.pallas_call(
        functools.partial(dispatch_kernel, inner=inner, top_k=top_k),
        out_shape=[jax.ShapeDtypeStruct((slots, width), jnp.bfloat16)] * inner
        + [table, table, jax.ShapeDtypeStruct((-(-inner // 8) * 8, LANES), jnp.float32)],
        in_specs=[pl.BlockSpec(memory_space=pltpu.SMEM), WHOLE],
        out_specs=[WHOLE] * (inner + 3),
        compiler_params=pltpu.CompilerParams(vmem_limit_bytes=SMALL_VMEM),
        cost_estimate=rows_cost(tokens, width),
    )(scalars, block)
    return list(outs[:inner]), outs[inner], outs[inner + 1], outs[inner + 2]


def pack_kernel(pack_ref, block_ref, *rows_refs):
    for j, rows_ref in enumerate(rows_refs):
        rows_ref[...] = jnp.dot(pack_ref[j], block_ref[...], preferred_element_type=jnp.float32).astype(jnp.bfloat16)


def pack_rows(pack, block):
    inner, slots, tokens = pack.shape
    width = block.shape[1]
    return list(
        pl.pallas_call(
            pack_kernel,
            out_shape=[jax.ShapeDtypeStruct((slots, width), jnp.bfloat16)] * inner,
            in_specs=[WHOLE] * 2,
            out_specs=[WHOLE] * inner,
            compiler_params=pltpu.CompilerParams(vmem_limit_bytes=SMALL_VMEM),
            cost_estimate=rows_cost(tokens, width),
        )(pack, block)
    )


def combine_kernel(combine_ref, *refs, inner, parts, carried):
    out_ref = refs[-1]
    width = refs[0].shape[1]
    for i in range(parts):
        total = refs[parts * inner + i][...].astype(jnp.float32) if carried else None
        for j in range(inner):
            part = lax.dot_general(
                combine_ref[j], refs[i * inner + j][...], (((0,), (0,)), ((), ())), preferred_element_type=jnp.float32
            )
            total = part if total is None else total + part
        out_ref[:, i * width : (i + 1) * width] = total.astype(jnp.bfloat16)


def combine_rows(table, rows, carried):
    inner, _, tokens = table.shape
    parts = len(rows)
    width = parts * rows[0][0].shape[1]
    flat = sum(rows, [])
    return pl.pallas_call(
        functools.partial(combine_kernel, inner=inner, parts=parts, carried=len(carried)),
        out_shape=jax.ShapeDtypeStruct((tokens, width), jnp.bfloat16),
        in_specs=[WHOLE] * (1 + len(flat) + len(carried)),
        out_specs=WHOLE,
        compiler_params=pltpu.CompilerParams(vmem_limit_bytes=SMALL_VMEM),
        cost_estimate=rows_cost(tokens, width),
    )(table, *flat, *carried)


def expert_kernel(*refs, pieces, chunks):
    count = pieces * PARTS
    row_refs, weights, out_refs = refs[:count], refs[count : count + 2], refs[count + 2 : 2 * count + 2]
    rows_scr, hidden_scr, own_scr, other_scr, up_sem, down_sem = refs[2 * count + 2 :]
    held = (own_scr, other_scr)
    slots = row_refs[0].shape[0]
    chunk = rows_scr.shape[2]

    def up_copy(half, k):
        part = (pl.ds(0, 2), pl.ds(k * chunk, chunk))
        return pltpu.make_async_copy(weights[half].at[part], held[half].at[part], up_sem.at[half, k])

    def down_copy(half, k):
        part = (pl.ds(2, 1), pl.ds(k * chunk, chunk))
        return pltpu.make_async_copy(weights[half].at[part], held[half].at[part], down_sem.at[half, k])

    for half in range(2):
        for k in range(chunks):
            up_copy(half, k).start()
    for k in range(chunks):
        for half in range(2):
            down_copy(half, k).start()
    for i in range(pieces):
        for k in range(chunks):
            part, k_in = divmod(k, chunks // PARTS)
            source = row_refs[i * PARTS + part]
            rows_scr[k, i * slots : (i + 1) * slots, :] = source[:, k_in * chunk : (k_in + 1) * chunk]
    for half in range(2):
        gate_act = up_act = None
        for k in range(chunks):
            up_copy(half, k).wait()
            rows = rows_scr[k]
            gate_part = jnp.dot(rows, held[half][0, k * chunk : (k + 1) * chunk], preferred_element_type=jnp.float32)
            up_part = jnp.dot(rows, held[half][1, k * chunk : (k + 1) * chunk], preferred_element_type=jnp.float32)
            gate_act = gate_part if k == 0 else gate_act + gate_part
            up_act = up_part if k == 0 else up_act + up_part
        hidden_scr[half] = (jax.nn.silu(gate_act) * up_act).astype(jnp.bfloat16)
    for k in range(chunks):
        out = None
        for half in range(2):
            down_copy(half, k).wait()
            part = lax.dot_general(
                hidden_scr[half],
                held[half][2, k * chunk : (k + 1) * chunk],
                (((1,), (1,)), ((), ())),
                preferred_element_type=jnp.float32,
            )
            out = part if half == 0 else out + part
        out = out.astype(jnp.bfloat16)
        for i in range(pieces):
            part, k_in = divmod(k, chunks // PARTS)
            target = out_refs[i * PARTS + part]
            target[:, k_in * chunk : (k_in + 1) * chunk] = out[i * slots : (i + 1) * slots]


def expert_rows(pieces, own, other):
    count = len(pieces)
    slots, part = pieces[0][0].shape
    units = own.shape[2]
    chunk = tile_of(part, CHUNK)
    chunks = PARTS * part // chunk
    rows = count * slots
    outs = pl.pallas_call(
        functools.partial(expert_kernel, pieces=count, chunks=chunks),
        out_shape=[jax.ShapeDtypeStruct((slots, part), jnp.bfloat16)] * (count * PARTS),
        in_specs=[WHOLE] * (count * PARTS) + [ANYWHERE] * 2,
        out_specs=[WHOLE] * (count * PARTS),
        scratch_shapes=[
            pltpu.VMEM((chunks, rows, chunk), jnp.bfloat16),
            pltpu.VMEM((2, rows, units), jnp.bfloat16),
            pltpu.VMEM(own.shape, jnp.bfloat16),
            pltpu.VMEM(own.shape, jnp.bfloat16),
            pltpu.SemaphoreType.DMA((2, chunks)),
            pltpu.SemaphoreType.DMA((2, chunks)),
        ],
        compiler_params=pltpu.CompilerParams(vmem_limit_bytes=VMEM_LIMIT),
        cost_estimate=pl.CostEstimate(
            flops=12 * rows * PARTS * part * units, bytes_accessed=4 * own.size, transcendentals=0
        ),
    )(*sum(pieces, []), own, other)
    return [list(outs[i * PARTS : (i + 1) * PARTS]) for i in range(count)]


def on_device(tokens, expert_weights, expert_ids, copy_ids, gate_weights):
    devices = lax.axis_size("expert")
    experts = devices // CORES
    outer, inner = grid_of(experts)
    tok_rows, top_k = expert_ids.shape
    slots = -(-2 * (tok_rows * top_k // experts) // 16) * 16
    me = lax.axis_index("expert").astype(jnp.int32)
    chip = lax.div(me, CORES)
    col = lax.rem(chip, inner)
    plane = lax.div(chip, inner)
    ring = ring_of(outer)

    def device_of(p, q, c):
        return (p * inner + q) * CORES + c

    every = [(p, q, c) for p in range(outer) for q in range(inner) for c in range(CORES)]

    def ring_pairs(shift):
        return [
            (device_of(p, q, c), device_of(ring[(ring.index(p) + shift) % outer], q, c)) for p, q, c in every
        ]

    def column_pairs(shift):
        return [(device_of(p, q, c), device_of(p, (q + shift) % inner, c)) for p, q, c in every]

    core_pairs = [(device_of(p, q, c), device_of(p, q, 1 - c)) for p, q, c in every]

    def permute(x, pairs):
        return lax.ppermute(x, "expert", pairs)

    scalars = jnp.stack([plane * inner, col])

    def behind(x, *others):
        return lax.optimization_barrier((x,) + others)[0] if others else x

    def swap(rows, sign):
        return rows[:1] + [permute(rows[shift], column_pairs(sign * shift)) for shift in range(1, inner)]

    def run(pieces):
        return expert_rows(pieces, expert_weights, other_weights)

    def transposed(lists):
        return [list(group) for group in zip(*lists)]

    last = outer - 1
    packs, tables, counts = [None] * outer, [None] * outer, [None] * outer
    packed = [[None] * PARTS for _ in range(outer)]
    sent = [[None] * PARTS for _ in range(outer)]
    results, back, sums = [None] * outer, [None] * outer, [None] * outer
    carry = [()] * PARTS

    def dispatch(step, i, block):
        if i == 0:
            packed[step][0], packs[step], tables[step], counts[step] = dispatch_rows(scalars, block, top_k, inner, slots)
        else:
            packed[step][i] = pack_rows(packs[step], block)
        sent[step][i] = swap(packed[step][i], 1)

    def give_back(step, *others, late=()):
        parts = transposed(results[step])
        parts[0] = parts[0][:1] + [behind(x, *others) for x in parts[0][1:]]
        parts[1:] = [part[:1] + [behind(x, *late) for x in part[1:]] for part in parts[1:]]
        back[step] = [swap(rows, -1) for rows in parts]

    def pass_on(step, gates, these=range(PARTS)):
        sums[step] = sums[step] or []
        for i in these:
            table = behind(tables[step], *gates[i])
            sums[step].append(combine_rows(table, [back[step][i]], carry[i]))
            carry[i] = (permute(sums[step][i], ring_pairs(1)),)

    none = ((),) * PARTS
    block = label_rows(tokens, expert_ids.T, copy_ids.T, gate_weights.T)
    other_weights = permute(expert_weights, core_pairs)
    for i in range(PARTS):
        dispatch(0, i, block[i])
    block = [permute(part, ring_pairs(1)) for part in block]
    for step in range(1, outer):
        onward = []
        for i in range(PARTS):
            here, gates = block[i], ()
            if step == 1 and i == 0:
                gates = tuple(sent[0][j][-1] for j in range(PARTS))
            if step == 2 and i == 1:
                pieces = transposed(sent[1])
                pieces[0][0] = behind(pieces[0][0], tables[2])
                results[1] = run(pieces)
                here = behind(here, results[1][0][0])
                gates = (results[1][0][0],)
            if step == 3 and i == 0:
                here = behind(here, sums[1][0])
            dispatch(step, i, here)
            if step == 1 and i > 0:
                gates = (packed[1][i][0], sent[1][i - 1][-1])
            if step < last:
                onward.append(permute(behind(block[i], *gates), ring_pairs(1)))
        block = onward
        if step == 2:
            give_back(1, sent[2][0][-1])
            pass_on(1, ((packed[2][-1][0],),) + none[1:], range(1))
    routes = sum(counts)
    routes = routes + permute(routes, core_pairs)
    served = routes[:1]
    for shift in range(1, inner):
        served = served + permute(routes[shift : shift + 1], column_pairs(shift))
    for step in range(2, outer):
        pieces = transposed(sent[step])
        if step == 2:
            gates = (sums[1][0], packed[3][0][0])
        else:
            gates = (sums[2][0],)
        pieces[0][0] = behind(pieces[0][0], *gates)
        if step == last:
            pieces = pieces + transposed(sent[0])
        results[step] = run(pieces)
        if step == 2:
            pass_on(1, none[:1] + ((results[2][0][0],),) * (PARTS - 1), range(1, PARTS))
        if step == last:
            results[0], results[step] = results[step][inner:], results[step][:inner]
        if step == 2:
            give_back(step, carry[0][0], sums[1][1], packed[3][-1][0], sent[3][0][-1], late=(sent[3][-1][-1],))
        else:
            give_back(step)
        pass_on(step, none)
    give_back(0, *(back[last][i][-1] for i in range(PARTS)))
    moe_out = combine_rows(tables[0], back[0], sum(carry, ()))

    return moe_out, served[:, :2].astype(jnp.int32)


def solution(mesh):
    return jax.shard_map(
        on_device,
        mesh=mesh,
        in_specs=(
            P(("groups", "expert"), None),
            P(None, None, "expert"),
            P(("groups", "expert"), None),
            P(("groups", "expert"), None),
            P(("groups", "expert"), None),
        ),
        out_specs=(P(("groups", "expert"), None), P(("groups", "expert"), None)),
        check_vma=False,
    )
```

```python
import functools

import jax
import jax.numpy as jnp
from jax import lax
from jax.experimental import pallas as pl
from jax.experimental.pallas import tpu as pltpu
from jax.sharding import PartitionSpec as P

CORES = 2
LANES = 128
PARTS = 2
LARGE_VMEM = 60 * 1024 * 1024
VMEM_LIMIT = 48 * 1024 * 1024
SMALL_VMEM = 16 * 1024 * 1024
CHUNK = 896


def grid_of(chips):
    inner = 1
    while (2 * inner) * (2 * inner) <= chips and chips % (2 * inner) == 0:
        inner *= 2
    return chips // inner, inner


def ring_of(length):
    return [p for p in range(length) if p % 2 == 0] + [p for p in reversed(range(length)) if p % 2 == 1]


def tile_of(size, most):
    tile = most
    while size % tile:
        tile -= 128
    return tile


ANYWHERE = pl.BlockSpec(memory_space=pl.ANY)
WHOLE = pl.BlockSpec(memory_space=pltpu.VMEM)


def rows_cost(rows, width):
    return pl.CostEstimate(flops=2 * rows * width, bytes_accessed=4 * rows * width, transcendentals=0)


def eye_of(size):
    row = lax.broadcasted_iota(jnp.int32, (size, size), 0)
    column = lax.broadcasted_iota(jnp.int32, (size, size), 1)
    return row, column


def label_kernel(tokens_ref, experts_ref, copies_ref, gates_ref, *refs):
    out_refs, (experts_scr, copies_scr, gates_scr, sem) = refs[:PARTS], refs[PARTS:]
    width = tokens_ref.shape[1] // PARTS
    top_k, tokens = experts_ref.shape
    moves = [
        pltpu.make_async_copy(experts_ref, experts_scr, sem.at[0]),
        pltpu.make_async_copy(copies_ref, copies_scr, sem.at[1]),
        pltpu.make_async_copy(gates_ref, gates_scr, sem.at[2]),
    ]
    for i in range(PARTS):
        part = tokens_ref.at[:, pl.ds(i * width, width)]
        moves.append(pltpu.make_async_copy(part, out_refs[i].at[:, pl.ds(0, width)], sem.at[3 + i]))
    for move in moves:
        move.start()
    for move in moves[:3]:
        move.wait()
    lane = lax.broadcasted_iota(jnp.int32, (LANES, tokens), 0)
    labels = jnp.zeros((LANES, tokens), jnp.float32)
    for k in range(top_k):
        for i, ref in enumerate((experts_scr, copies_scr, gates_scr)):
            values = jnp.broadcast_to(ref[k : k + 1, :].astype(jnp.float32), (LANES, tokens))
            labels = jnp.where(lane == i * top_k + k, values, labels)
    row, column = eye_of(LANES)
    eye = jnp.where(row == column, 1.0, 0.0).astype(jnp.bfloat16)
    turned = lax.dot_general(
        labels.astype(jnp.bfloat16), eye, (((0,), (0,)), ((), ())), preferred_element_type=jnp.float32
    )
    out_refs[0][:, width:] = turned.astype(jnp.bfloat16)
    for move in moves[3:]:
        move.wait()


def label_rows(tokens, experts, copies, gates):
    rows, width = tokens.shape
    part = width // PARTS
    return list(
        pl.pallas_call(
            label_kernel,
            out_shape=[
                jax.ShapeDtypeStruct((rows, part + (0 if i else LANES)), jnp.bfloat16) for i in range(PARTS)
            ],
            in_specs=[ANYWHERE] * 4,
            out_specs=[WHOLE] * PARTS,
            scratch_shapes=[
                pltpu.VMEM(experts.shape, experts.dtype),
                pltpu.VMEM(copies.shape, copies.dtype),
                pltpu.VMEM(gates.shape, gates.dtype),
                pltpu.SemaphoreType.DMA((3 + PARTS,)),
            ],
            compiler_params=pltpu.CompilerParams(vmem_limit_bytes=LARGE_VMEM),
            cost_estimate=rows_cost(rows, width),
        )(tokens, experts, copies, gates)
    )


def dispatch_kernel(scalars, block_ref, *refs, inner, top_k):
    rows_refs, (pack_ref, combine_ref, counts_ref) = refs[:inner], refs[inner:]
    tokens = block_ref.shape[0]
    slots, width = rows_refs[0].shape
    base, col = scalars[0], scalars[1]
    row, column = eye_of(tokens)
    eye = jnp.where(row == column, 1.0, 0.0).astype(jnp.bfloat16)
    upto = jnp.where(row <= column, 1.0, 0.0).astype(jnp.bfloat16)
    labels = lax.dot_general(
        block_ref[:, width:], eye, (((0,), (0,)), ((), ())), preferred_element_type=jnp.float32
    )
    slot = lax.broadcasted_iota(jnp.int32, (slots, tokens), 0)
    lane = lax.broadcasted_iota(jnp.int32, (1, LANES), 1)
    counts_ref[...] = jnp.zeros_like(counts_ref)
    for j in range(inner):
        wanted = (base + lax.rem(col + j, inner)).astype(jnp.float32)
        hit = jnp.zeros((1, tokens), jnp.float32)
        weight = jnp.zeros((1, tokens), jnp.float32)
        upper = jnp.zeros((1, tokens), jnp.float32)
        for k in range(top_k):
            same = labels[k : k + 1] == wanted
            hit = hit + jnp.where(same, 1.0, 0.0)
            upper = upper + jnp.where(same, labels[top_k + k : top_k + k + 1], 0.0)
            weight = weight + jnp.where(same, labels[2 * top_k + k : 2 * top_k + k + 1], 0.0)
        wide = jnp.broadcast_to(hit, (8, tokens)).astype(jnp.bfloat16)
        rank = jnp.dot(wide, upto, preferred_element_type=jnp.float32)[:1].astype(jnp.int32) - 1
        chosen = (slot == rank) & (hit > 0.5)
        pack = jnp.where(chosen, 1.0, 0.0).astype(jnp.bfloat16)
        pack_ref[j] = pack
        combine_ref[j] = jnp.where(chosen, weight, 0.0).astype(jnp.bfloat16)
        rows_refs[j][...] = jnp.dot(pack, block_ref[:, :width], preferred_element_type=jnp.float32).astype(jnp.bfloat16)
        ones = jnp.sum(upper, axis=1, keepdims=True)
        zeros = jnp.sum(hit, axis=1, keepdims=True) - ones
        counts_ref[j : j + 1, :] = jnp.where(lane == 0, zeros, jnp.where(lane == 1, ones, 0.0))


def dispatch_rows(scalars, block, top_k, inner, slots):
    tokens, width = block.shape
    width -= LANES
    table = jax.ShapeDtypeStruct((inner, slots, tokens), jnp.bfloat16)
    outs = pl.pallas_call(
        functools.partial(dispatch_kernel, inner=inner, top_k=top_k),
        out_shape=[jax.ShapeDtypeStruct((slots, width), jnp.bfloat16)] * inner
        + [table, table, jax.ShapeDtypeStruct((-(-inner // 8) * 8, LANES), jnp.float32)],
        in_specs=[pl.BlockSpec(memory_space=pltpu.SMEM), WHOLE],
        out_specs=[WHOLE] * (inner + 3),
        compiler_params=pltpu.CompilerParams(vmem_limit_bytes=SMALL_VMEM),
        cost_estimate=rows_cost(tokens, width),
    )(scalars, block)
    return list(outs[:inner]), outs[inner], outs[inner + 1], outs[inner + 2]


def pack_kernel(pack_ref, block_ref, *rows_refs):
    for j, rows_ref in enumerate(rows_refs):
        rows_ref[...] = jnp.dot(pack_ref[j], block_ref[...], preferred_element_type=jnp.float32).astype(jnp.bfloat16)


def pack_rows(pack, block):
    inner, slots, tokens = pack.shape
    width = block.shape[1]
    return list(
        pl.pallas_call(
            pack_kernel,
            out_shape=[jax.ShapeDtypeStruct((slots, width), jnp.bfloat16)] * inner,
            in_specs=[WHOLE] * 2,
            out_specs=[WHOLE] * inner,
            compiler_params=pltpu.CompilerParams(vmem_limit_bytes=SMALL_VMEM),
            cost_estimate=rows_cost(tokens, width),
        )(pack, block)
    )


def combine_kernel(combine_ref, *refs, inner, parts, carried):
    out_ref = refs[-1]
    width = refs[0].shape[1]
    for i in range(parts):
        total = refs[parts * inner + i][...].astype(jnp.float32) if carried else None
        for j in range(inner):
            part = lax.dot_general(
                combine_ref[j], refs[i * inner + j][...], (((0,), (0,)), ((), ())), preferred_element_type=jnp.float32
            )
            total = part if total is None else total + part
        out_ref[:, i * width : (i + 1) * width] = total.astype(jnp.bfloat16)


def combine_rows(table, rows, carried):
    inner, _, tokens = table.shape
    parts = len(rows)
    width = parts * rows[0][0].shape[1]
    flat = sum(rows, [])
    return pl.pallas_call(
        functools.partial(combine_kernel, inner=inner, parts=parts, carried=len(carried)),
        out_shape=jax.ShapeDtypeStruct((tokens, width), jnp.bfloat16),
        in_specs=[WHOLE] * (1 + len(flat) + len(carried)),
        out_specs=WHOLE,
        compiler_params=pltpu.CompilerParams(vmem_limit_bytes=SMALL_VMEM),
        cost_estimate=rows_cost(tokens, width),
    )(table, *flat, *carried)


def expert_kernel(*refs, pieces, chunks):
    count = pieces * PARTS
    row_refs, weights, out_refs = refs[:count], refs[count : count + 2], refs[count + 2 : 2 * count + 2]
    rows_scr, hidden_scr, own_scr, other_scr, up_sem, down_sem = refs[2 * count + 2 :]
    held = (own_scr, other_scr)
    slots = row_refs[0].shape[0]
    chunk = rows_scr.shape[2]

    def up_copy(half, k):
        part = (pl.ds(0, 2), pl.ds(k * chunk, chunk))
        return pltpu.make_async_copy(weights[half].at[part], held[half].at[part], up_sem.at[half, k])

    def down_copy(half, k):
        part = (pl.ds(2, 1), pl.ds(k * chunk, chunk))
        return pltpu.make_async_copy(weights[half].at[part], held[half].at[part], down_sem.at[half, k])

    for half in range(2):
        for k in range(chunks):
            up_copy(half, k).start()
    for k in range(chunks):
        for half in range(2):
            down_copy(half, k).start()
    for i in range(pieces):
        for k in range(chunks):
            part, k_in = divmod(k, chunks // PARTS)
            source = row_refs[i * PARTS + part]
            rows_scr[k, i * slots : (i + 1) * slots, :] = source[:, k_in * chunk : (k_in + 1) * chunk]
    for half in range(2):
        gate_act = up_act = None
        for k in range(chunks):
            up_copy(half, k).wait()
            rows = rows_scr[k]
            gate_part = jnp.dot(rows, held[half][0, k * chunk : (k + 1) * chunk], preferred_element_type=jnp.float32)
            up_part = jnp.dot(rows, held[half][1, k * chunk : (k + 1) * chunk], preferred_element_type=jnp.float32)
            gate_act = gate_part if k == 0 else gate_act + gate_part
            up_act = up_part if k == 0 else up_act + up_part
        hidden_scr[half] = (jax.nn.silu(gate_act) * up_act).astype(jnp.bfloat16)
    for k in range(chunks):
        out = None
        for half in range(2):
            down_copy(half, k).wait()
            part = lax.dot_general(
                hidden_scr[half],
                held[half][2, k * chunk : (k + 1) * chunk],
                (((1,), (1,)), ((), ())),
                preferred_element_type=jnp.float32,
            )
            out = part if half == 0 else out + part
        out = out.astype(jnp.bfloat16)
        for i in range(pieces):
            part, k_in = divmod(k, chunks // PARTS)
            target = out_refs[i * PARTS + part]
            target[:, k_in * chunk : (k_in + 1) * chunk] = out[i * slots : (i + 1) * slots]


def expert_rows(pieces, own, other):
    count = len(pieces)
    slots, part = pieces[0][0].shape
    units = own.shape[2]
    chunk = tile_of(part, CHUNK)
    chunks = PARTS * part // chunk
    rows = count * slots
    outs = pl.pallas_call(
        functools.partial(expert_kernel, pieces=count, chunks=chunks),
        out_shape=[jax.ShapeDtypeStruct((slots, part), jnp.bfloat16)] * (count * PARTS),
        in_specs=[WHOLE] * (count * PARTS) + [ANYWHERE] * 2,
        out_specs=[WHOLE] * (count * PARTS),
        scratch_shapes=[
            pltpu.VMEM((chunks, rows, chunk), jnp.bfloat16),
            pltpu.VMEM((2, rows, units), jnp.bfloat16),
            pltpu.VMEM(own.shape, jnp.bfloat16),
            pltpu.VMEM(own.shape, jnp.bfloat16),
            pltpu.SemaphoreType.DMA((2, chunks)),
            pltpu.SemaphoreType.DMA((2, chunks)),
        ],
        compiler_params=pltpu.CompilerParams(vmem_limit_bytes=VMEM_LIMIT),
        cost_estimate=pl.CostEstimate(
            flops=12 * rows * PARTS * part * units, bytes_accessed=4 * own.size, transcendentals=0
        ),
    )(*sum(pieces, []), own, other)
    return [list(outs[i * PARTS : (i + 1) * PARTS]) for i in range(count)]


def on_device(tokens, expert_weights, expert_ids, copy_ids, gate_weights):
    devices = lax.axis_size("expert")
    experts = devices // CORES
    outer, inner = grid_of(experts)
    tok_rows, top_k = expert_ids.shape
    slots = -(-2 * (tok_rows * top_k // experts) // 16) * 16
    me = lax.axis_index("expert").astype(jnp.int32)
    chip = lax.div(me, CORES)
    col = lax.rem(chip, inner)
    plane = lax.div(chip, inner)
    ring = ring_of(outer)

    def device_of(p, q, c):
        return (p * inner + q) * CORES + c

    every = [(p, q, c) for p in range(outer) for q in range(inner) for c in range(CORES)]

    def ring_pairs(shift):
        return [
            (device_of(p, q, c), device_of(ring[(ring.index(p) + shift) % outer], q, c)) for p, q, c in every
        ]

    def column_pairs(shift):
        return [(device_of(p, q, c), device_of(p, (q + shift) % inner, c)) for p, q, c in every]

    core_pairs = [(device_of(p, q, c), device_of(p, q, 1 - c)) for p, q, c in every]

    def permute(x, pairs):
        return lax.ppermute(x, "expert", pairs)

    scalars = jnp.stack([plane * inner, col])

    def behind(x, *others):
        return lax.optimization_barrier((x,) + others)[0] if others else x

    def swap(rows, sign):
        return rows[:1] + [permute(rows[shift], column_pairs(sign * shift)) for shift in range(1, inner)]

    def run(pieces):
        return expert_rows(pieces, expert_weights, other_weights)

    def transposed(lists):
        return [list(group) for group in zip(*lists)]

    last = outer - 1
    packs, tables, counts = [None] * outer, [None] * outer, [None] * outer
    packed = [[None] * PARTS for _ in range(outer)]
    sent = [[None] * PARTS for _ in range(outer)]
    results, back, sums = [None] * outer, [None] * outer, [None] * outer
    carry = [()] * PARTS

    def dispatch(step, i, block):
        if i == 0:
            packed[step][0], packs[step], tables[step], counts[step] = dispatch_rows(scalars, block, top_k, inner, slots)
        else:
            packed[step][i] = pack_rows(packs[step], block)
        sent[step][i] = swap(packed[step][i], 1)

    def give_back(step, *others, late=()):
        parts = transposed(results[step])
        parts[0] = parts[0][:1] + [behind(x, *others) for x in parts[0][1:]]
        parts[1:] = [part[:1] + [behind(x, *late) for x in part[1:]] for part in parts[1:]]
        back[step] = [swap(rows, -1) for rows in parts]

    def pass_on(step, gates, these=range(PARTS)):
        sums[step] = sums[step] or []
        for i in these:
            table = behind(tables[step], *gates[i])
            sums[step].append(combine_rows(table, [back[step][i]], carry[i]))
            carry[i] = (permute(sums[step][i], ring_pairs(1)),)

    none = ((),) * PARTS
    block = label_rows(tokens, expert_ids.T, copy_ids.T, gate_weights.T)
    other_weights = permute(behind(expert_weights, block[0]), core_pairs)
    for i in range(PARTS):
        dispatch(0, i, block[i])
    block = [permute(part, ring_pairs(1)) for part in block]
    for step in range(1, outer):
        onward = []
        for i in range(PARTS):
            here, gates = block[i], ()
            if step == 1 and i == 0:
                gates = tuple(sent[0][j][-1] for j in range(PARTS))
            if step == 2 and i == 1:
                pieces = transposed(sent[1])
                pieces[0][0] = behind(pieces[0][0], tables[2])
                results[1] = run(pieces)
                here = behind(here, results[1][0][0])
                gates = (results[1][0][0],)
            if step == 3 and i == 0:
                here = behind(here, sums[1][0])
            dispatch(step, i, here)
            if step == 1 and i > 0:
                gates = (packed[1][i][0], sent[1][i - 1][-1])
            if step < last:
                onward.append(permute(behind(block[i], *gates), ring_pairs(1)))
        block = onward
        if step == 2:
            give_back(1, sent[2][0][-1])
            pass_on(1, ((packed[2][-1][0],),) + none[1:], range(1))
    routes = sum(counts)
    routes = routes + permute(routes, core_pairs)
    served = routes[:1]
    for shift in range(1, inner):
        served = served + permute(routes[shift : shift + 1], column_pairs(shift))
    for step in range(2, outer):
        pieces = transposed(sent[step])
        if step == 2:
            gates = (sums[1][0], packed[3][0][0])
        else:
            gates = (sums[2][0],)
        pieces[0][0] = behind(pieces[0][0], *gates)
        if step == last:
            pieces = pieces + transposed(sent[0])
        results[step] = run(pieces)
        if step == 2:
            pass_on(1, none[:1] + ((results[2][0][0],),) * (PARTS - 1), range(1, PARTS))
        if step == last:
            results[0], results[step] = results[step][inner:], results[step][:inner]
        if step == 2:
            give_back(step, carry[0][0], sums[1][1], packed[3][-1][0], sent[3][0][-1], late=(sent[3][-1][-1],))
        else:
            give_back(step)
        pass_on(step, none)
    give_back(0, back[last][0][-1], late=(back[last][0][-1],))
    moe_out = combine_rows(tables[0], back[0], sum(carry, ()))

    return moe_out, served[:, :2].astype(jnp.int32)


def solution(mesh):
    return jax.shard_map(
        on_device,
        mesh=mesh,
        in_specs=(
            P(("groups", "expert"), None),
            P(None, None, "expert"),
            P(("groups", "expert"), None),
            P(("groups", "expert"), None),
            P(("groups", "expert"), None),
        ),
        out_specs=(P(("groups", "expert"), None), P(("groups", "expert"), None)),
        check_vma=False,
    )
```
